32 devices in a mesh: col: 4 (over z), grp: 8 (over y, x, core).
Axes of the slice: x: 2, y: 2, z: 4, core: 2. Of those that a mesh axis runs over, the one named last changes fastest.
Arguments:
- table_rows: bfloat16 [8, 256, 256], P('grp', None, 'col'), may hold values from -1.5 to 1.5
- pool_index: int32 [8, 4, 1024], P('grp'), may hold values from 0 to 255
- bag_length: int32 [8, 1024], P('grp'), may hold values from 1 to 4
- table_slot: int32 [8], replicated, may hold values from 0 to 7, each once
- dense_input: bfloat16 [1024, 13], P('grp'), may hold values from -6 to 6
- bottom_weight: bfloat16 [13, 256], replicated, may hold values from -1.75 to 1.75
- top_weight: bfloat16 [292, 2048], P(None, 'col'), may hold values from -0.375 to 0.375
- out_weight: bfloat16 [2048], P('col'), may hold values from -0.125 to 0.125
- labels: int32 [1024], P('grp'), may hold values 0 or 1
Outputs:
- logits: float32 [1024], P('grp')
- grad_top: float32 [292, 2048], P(None, ('col', 'grp'))
- grad_out: float32 [2048], P(('col', 'grp'))
- grad_bottom: float32 [13, 256], replicated
- grad_rows: float32 [8, 256, 256], P('grp', None, 'col')
The draws below stay inside these ranges and needn't reach their ends.
Inputs may be any that keep to these rules, and one draw needn't show every extreme that they name: `pool_index`: each entry names one of its table's 256 looked-up rows. `bag_length`: slots at or past a bag's length are unused. `table_slot`: every feature is held by exactly one shard.
All inputs are finite; a program needn't handle non-finite values. No bound on the sum of `labels` on one device may be relied on, other than what follows from the above.
Results may differ from the reference program's by a relative error of at most 0.0071.
Values may be sent and summed in bfloat16 or wider, within the bound.
A program may use at most 128 MiB of HBM per device.

```python
import math
import jax
import jax.numpy as jnp
import numpy as np
from jax import lax

D_EMB = 256
HID = 2048
DENSE = 13
BAG = 4
UNIQ = 256
SAMP_DEV = 128
TABLES = 8
SAMPLES = 1024
TOPIN = 292


def with_ends(drawn, own_key, least, largest):
    longest = drawn.shape.index(max(drawn.shape))
    spots = []
    for shift in (0, 1):
        where = [jax.random.randint(jax.random.fold_in(own_key, axis), (), 0, length) for axis, length in enumerate(drawn.shape)]
        where[longest] = (where[longest] + shift) % drawn.shape[longest]
        spots.append(tuple(where))
    return drawn.at[spots[0]].set(least).at[spots[1]].set(largest)


def block_levels(own_key, extent, shards, least, high):
    loudness = 1.0
    for dim, blocks in shards:
        heights = jax.random.uniform(jax.random.fold_in(jax.random.fold_in(own_key, 6), dim), (blocks,), jnp.float32, least / len(shards), high / len(shards))
        loudness = loudness * jnp.repeat(jnp.exp(heights), extent[dim] // blocks).reshape((-1,) + (1,) * (len(extent) - 1 - dim))
    return loudness


def cumulative_ranks(number_of, lean):
    portions = [(1 << 20) // math.isqrt(rank ** lean) + 1 for rank in range(1, number_of + 1)]
    spread = 1 + sum(portions) // (1 << 30)
    return np.cumsum(np.array([max(1, weight // spread) for weight in portions]))


def ranked(own_key, dims, count, skew):
    table = cumulative_ranks(count, skew)
    ticket = jax.random.randint(jax.random.fold_in(own_key, 1), dims, 0, int(table[count - 1]))
    standing = jnp.searchsorted(jnp.asarray(table, jnp.int32), ticket, side="right")
    return jax.random.permutation(jax.random.fold_in(own_key, 2), count)[standing].astype(jnp.int32)


def normal_values(rng, dims, width, limit, shards=(), dtype=jnp.bfloat16):
    gain = block_levels(rng, dims, shards, -0.22, 0.18) if shards else 1.0
    entries = jax.random.normal(rng, dims, jnp.float32) * width * gain
    return jnp.minimum(jnp.maximum(entries, -limit), limit).astype(dtype)


def setup_inputs(seed: int = 0) -> dict:
    seeds = jax.random.split(jax.random.key(seed), 10)
    return {
        "table_rows": normal_values(seeds[0], (TABLES, UNIQ, D_EMB), 0.25, 1.5, ((0, 8), (2, 4))),
        "pool_index": with_ends(ranked(seeds[1], (TABLES, BAG, SAMPLES), UNIQ, 2), jax.random.fold_in(seeds[1], 3), 0, UNIQ - 1).astype(jnp.int32),
        "bag_length": with_ends(jax.random.randint(seeds[2], (TABLES, SAMPLES), 1, BAG + 1), jax.random.fold_in(seeds[2], 1), 1, BAG).astype(jnp.int32),
        "table_slot": jax.random.permutation(seeds[3], TABLES).astype(jnp.int32),
        "dense_input": normal_values(seeds[4], (SAMPLES, DENSE), 1.0, 6.0, ((0, 8),)),
        "bottom_weight": normal_values(seeds[5], (DENSE, D_EMB), DENSE ** -0.5, 1.75),
        "top_weight": normal_values(seeds[6], (TOPIN, HID), TOPIN ** -0.5, 0.375, ((1, 4),)),
        "out_weight": normal_values(seeds[7], (HID,), HID ** -0.5, 0.125, ((0, 4),)),
        "labels": with_ends((jax.random.randint(seeds[8], (SAMPLES,), 0, 2) < 1).astype(jnp.int32), jax.random.fold_in(seeds[8], 1), 0, 1),
    }


def pair_table(fields):
    upper_a, upper_b = np.triu_indices(fields, 1)
    return upper_a * fields + upper_b


def silu_slope(values):
    sigma = jax.nn.sigmoid(values)
    return sigma * (1.0 + values * (1.0 - sigma))


def reference(table_rows, pool_index, bag_length, table_slot, dense_input, bottom_weight, top_weight, out_weight, labels):
    def pool_one(inputs):
        table_block, index_block, length_block = inputs
        active = (lax.broadcasted_iota(jnp.int32, index_block.shape, 0) < length_block[None, :]).astype(jnp.float32)
        picked = table_block.astype(jnp.float32)[index_block]
        return jnp.sum(picked * active[:, :, None], axis=0).astype(jnp.bfloat16)

    pooled = lax.map(pool_one, (table_rows, pool_index, bag_length))
    bottom_pre = jnp.dot(dense_input, bottom_weight, preferred_element_type=jnp.float32)
    bottom_out = jax.nn.silu(bottom_pre).astype(jnp.bfloat16)
    inverse = jnp.argsort(table_slot).astype(jnp.int32)
    vectors = jnp.concatenate([bottom_out[None], jnp.take(pooled, inverse, axis=0)], axis=0)
    fields = vectors.shape[0]
    pair_flat = pair_table(fields)
    wide_vectors = vectors.astype(jnp.float32)
    gram_matrix = jnp.einsum("asc,bsc->abs", wide_vectors, wide_vectors)
    pair_values = gram_matrix.reshape(fields * fields, -1)[pair_flat]
    features = jnp.concatenate([bottom_out.astype(jnp.float32), pair_values.T], axis=1).astype(jnp.bfloat16)
    hidden_pre = jnp.dot(features, top_weight, preferred_element_type=jnp.float32)
    hidden = jax.nn.silu(hidden_pre).astype(jnp.bfloat16)
    logits = jnp.dot(hidden, out_weight, preferred_element_type=jnp.float32)
    dlogit = (jax.nn.sigmoid(logits) - labels.astype(jnp.float32)) / SAMP_DEV
    grad_out = jnp.dot(hidden.astype(jnp.float32).T, dlogit, precision=lax.Precision.HIGHEST)
    out_delta = (dlogit[:, None] * out_weight.astype(jnp.float32)[None, :] * silu_slope(hidden_pre)).astype(jnp.bfloat16)
    grad_top = jnp.dot(features.T, out_delta, preferred_element_type=jnp.float32)
    dfeatures = jnp.dot(out_delta, top_weight.T, preferred_element_type=jnp.float32)
    dpairs = dfeatures[:, D_EMB:].astype(jnp.bfloat16)
    symmetric = jnp.zeros((fields * fields, dpairs.shape[0]), jnp.bfloat16).at[pair_flat].set(dpairs.T)
    symmetric = symmetric.reshape(fields, fields, -1)
    symmetric = symmetric + jnp.transpose(symmetric, (1, 0, 2))
    dvectors = jnp.einsum("abs,bsc->asc", symmetric.astype(jnp.float32), wide_vectors)
    dbottom = (dfeatures[:, :D_EMB] + dvectors[0]) * silu_slope(bottom_pre)
    grad_bottom = jnp.dot(dense_input.astype(jnp.float32).T, dbottom, precision=lax.Precision.HIGHEST)
    dpooled = jnp.take(dvectors[1:], table_slot, axis=0).astype(jnp.bfloat16)

    def grads_one(inputs):
        index_block, length_block, grad_block = inputs
        active = lax.broadcasted_iota(jnp.int32, index_block.shape, 0) < length_block[None, :]
        row_ids = jnp.where(active, index_block, 0).reshape(-1)
        weights = active.astype(jnp.float32)[:, :, None] * grad_block.astype(jnp.float32)[None]
        return jax.ops.segment_sum(weights.reshape(-1, weights.shape[2]), row_ids, num_segments=UNIQ)

    grad_rows = lax.map(grads_one, (pool_index, bag_length, dpooled))
    return logits, grad_top, grad_out, grad_bottom, grad_rows
```

```python
import functools

import jax
import jax.numpy as jnp
import numpy as np
from jax import lax
from jax.experimental import pallas as pl
from jax.experimental.pallas import tpu as pltpu
from jax.sharding import PartitionSpec as P


def count_block(index_block, length_block, uniq_count):
    slot_iota = lax.broadcasted_iota(jnp.int32, index_block.shape, 1)
    row_ids = jnp.where(slot_iota < length_block[:, None, :], index_block, -1)
    values = lax.broadcasted_iota(jnp.int32, (1, 1, uniq_count), 2)
    counts = jnp.zeros((index_block.shape[0], index_block.shape[2], uniq_count), jnp.bfloat16)
    for slot_index in range(index_block.shape[1]):
        counts = counts + jnp.where(row_ids[:, slot_index, :, None] == values, 1.0, 0.0).astype(
            jnp.bfloat16
        )
    return counts


def pair_table(fields):
    upper_a, upper_b = np.triu_indices(fields, 1)
    return upper_a * fields + upper_b


def silu_slope(values):
    sigma = jax.nn.sigmoid(values)
    return sigma * (1.0 + values * (1.0 - sigma))


def interact(vectors):
    fields = vectors.shape[0]
    gram_matrix = jnp.einsum("asc,bsc->abs", vectors, vectors, preferred_element_type=jnp.float32)
    return gram_matrix.reshape(fields * fields, -1)[pair_table(fields)]


def spread(dpairs, vectors):
    fields = vectors.shape[0]
    symmetric = (
        jnp.zeros((fields * fields, dpairs.shape[0]), jnp.bfloat16)
        .at[pair_table(fields)]
        .set(dpairs.T)
    )
    symmetric = symmetric.reshape(fields, fields, -1)
    symmetric = symmetric + jnp.transpose(symmetric, (1, 0, 2))
    return jnp.einsum("abs,bsc->asc", symmetric, vectors, preferred_element_type=jnp.float32)


def body(
    table_rows,
    pool_index,
    bag_length,
    table_slot,
    dense_input,
    bottom_weight,
    top_weight,
    out_weight,
    labels,
):
    tab_count, uniq_count, col_width = table_rows.shape
    bag_slots = pool_index.shape[1]
    samples = pool_index.shape[2]
    local_rows = dense_input.shape[0]
    emb_width = bottom_weight.shape[1]
    stride = min(1024, samples)
    nblocks = samples // stride
    index_blocks = jnp.transpose(
        pool_index.reshape(tab_count, bag_slots, nblocks, stride), (2, 0, 1, 3)
    )
    length_blocks = jnp.transpose(bag_length.reshape(tab_count, nblocks, stride), (1, 0, 2))

    def pool_one(inputs):
        counts = count_block(inputs[0], inputs[1], uniq_count)
        return jnp.einsum(
            "tbu,tuc->tbc", counts, table_rows, preferred_element_type=jnp.float32
        ).astype(jnp.bfloat16)

    pooled_blocks = lax.map(pool_one, (index_blocks, length_blocks))
    pooled = jnp.transpose(pooled_blocks, (1, 0, 2, 3)).reshape(tab_count, samples, col_width)
    picks = (
        lax.broadcasted_iota(jnp.int32, (table_slot.shape[0],) * 2, 0) == table_slot[None, :]
    ).astype(jnp.bfloat16)
    bottom_pre = jnp.dot(dense_input, bottom_weight, preferred_element_type=jnp.float32)
    bottom_out = jax.nn.silu(bottom_pre).astype(jnp.bfloat16)
    arrived = lax.all_to_all(pooled, "grp", split_axis=1, concat_axis=0, tiled=True)
    gathered = lax.all_gather(arrived, "col", axis=2, tiled=True)
    tables = jnp.einsum(
        "fk,ksc->fsc", picks, gathered, preferred_element_type=jnp.float32
    ).astype(jnp.bfloat16)
    mine_pre, mine_out, mine_dense = (bottom_pre, bottom_out, dense_input)
    vectors = jnp.concatenate([mine_out[None], tables], axis=0)
    pair_values = interact(vectors)
    features = jnp.concatenate([mine_out.astype(jnp.float32), pair_values.T], axis=1).astype(
        jnp.bfloat16
    )
    hidden_pre = jnp.dot(features, top_weight, preferred_element_type=jnp.float32)
    hidden = jax.nn.silu(hidden_pre).astype(jnp.bfloat16)
    logits = lax.psum(jnp.dot(hidden, out_weight, preferred_element_type=jnp.float32), "col")
    dlogit = (jax.nn.sigmoid(logits) - labels.astype(jnp.float32)) / local_rows
    grad_out_part = jnp.dot(hidden.astype(jnp.float32).T, dlogit, precision=lax.Precision.HIGHEST)
    out_delta = (
        dlogit[:, None] * out_weight.astype(jnp.float32)[None, :] * silu_slope(hidden_pre)
    ).astype(jnp.bfloat16)
    grad_top_part = lax.dot_general(
        features, out_delta, (((0,), (0,)), ((), ())), preferred_element_type=jnp.float32
    )
    grad_top, grad_out = (
        lax.psum_scatter(grad_top_part, "grp", scatter_dimension=1, tiled=True),
        lax.psum_scatter(grad_out_part, "grp", scatter_dimension=0, tiled=True),
    )
    dfeatures = lax.psum(
        lax.dot_general(
            out_delta, top_weight, (((1,), (1,)), ((), ())), preferred_element_type=jnp.float32
        ),
        "col",
    )
    dpairs = dfeatures[:, emb_width:].astype(jnp.bfloat16)
    dvectors = spread(dpairs, vectors)
    dbottom = (dfeatures[:, :emb_width] + dvectors[0]) * silu_slope(mine_pre)
    bottom_part = jnp.dot(
        mine_dense.astype(jnp.float32).T, dbottom, precision=lax.Precision.HIGHEST
    )
    dtables = jnp.einsum(
        "fk,fsc->ksc",
        picks,
        dvectors[1:].astype(jnp.bfloat16),
        preferred_element_type=jnp.float32,
    )
    grad_bottom = lax.psum(bottom_part, "grp")
    own_cols = lax.dynamic_slice_in_dim(
        dtables, lax.axis_index("col") * col_width, col_width, 2
    ).astype(jnp.bfloat16)
    dpooled = lax.all_to_all(own_cols, "grp", split_axis=0, concat_axis=1, tiled=True)
    dpooled_blocks = jnp.transpose(
        dpooled.reshape(tab_count, nblocks, stride, col_width), (1, 0, 2, 3)
    )

    def accumulate(running, inputs):
        counts = count_block(inputs[0], inputs[1], uniq_count)
        return (
            running
            + jnp.einsum("tbu,tbc->tuc", counts, inputs[2], preferred_element_type=jnp.float32),
            None,
        )

    grad_rows, _ = lax.scan(
        accumulate,
        jnp.zeros((tab_count, uniq_count, col_width), jnp.float32),
        (index_blocks, length_blocks, dpooled_blocks),
    )
    return (logits, grad_top, grad_out, grad_bottom, grad_rows)


MESH = pl.DeviceIdType.MESH
F32, BF16 = jnp.float32, jnp.bfloat16
UNROLLED_PAIRS = 128


def contract(left, right, left_dim, right_dim):
    return lax.dot_general(
        left, right, (((left_dim,), (right_dim,)), ((), ())), preferred_element_type=F32
    )


def up(count, unit):
    return -(-count // unit) * unit


def side_by_side(ref, count, rows):
    return jnp.concatenate([ref[k, rows, :] for k in range(count)], axis=1)


def split_rows(values, parts):
    row = lax.broadcasted_iota(jnp.int32, (16, values.shape[1]), 0)
    block = jnp.zeros((16, values.shape[1]), F32)
    rest = values
    for part in range(parts):
        head = rest.astype(BF16).astype(F32)
        block = jnp.where(row == part, head, block)
        rest = rest - head
    return block.astype(BF16)


def kernel(
    ncol, ngrp,
    slot_ref, rows_ref, index_ref, length_ref, dense_ref, bottom_ref, top_ref, out_ref, label_ref,
    logits_ref, grad_top_ref, grad_out_ref, grad_bottom_ref, grad_rows_ref,
    counts, pool_out, pool_in, weight_pad, pre, bottoms, base, spread_out, vec, gram_in,
    hid, logit_in, top_out, top_in, delta_out, delta_in, dvec, back_out, back_in, corner_in,
    pool_s, pool_r, gram_s, gram_r, logit_s, logit_r, top_s, top_r,
    delta_s, delta_r, back_s, back_r, corner_s, corner_r,
):
    col, grp = lax.axis_index("col"), lax.axis_index("grp")
    uniq, width = rows_ref.shape[1], rows_ref.shape[2]
    bag, samples = index_ref.shape[1], index_ref.shape[2]
    local, dense = dense_ref.shape
    emb = bottom_ref.shape[1]
    hidden_count = top_ref.shape[1]
    piece = hidden_count // ngrp
    fields = ngrp + 1
    pairs = [(a, b) for a in range(fields) for b in range(a + 1, fields)]
    npairs = len(pairs)
    pair_pad = up(npairs, 16)
    dense_pad = up(dense, 16)

    barrier = pltpu.get_barrier_semaphore()
    for d in range(1, ngrp):
        pl.semaphore_signal(
            barrier, inc=1, device_id={"grp": lax.rem(grp + d, ngrp)}, device_id_type=MESH
        )
    for d in range(1, ncol):
        pl.semaphore_signal(
            barrier, inc=1, device_id={"col": lax.rem(col + d, ncol)}, device_id_type=MESH
        )

    def send(axis, count, here, source, target, send_sem, recv_sem):
        copies = []
        for d in range(1, count):
            peer = lax.rem(here + d, count)
            copy = pltpu.make_async_remote_copy(
                src_ref=source(peer),
                dst_ref=target.at[here],
                send_sem=send_sem.at[d],
                recv_sem=recv_sem.at[d],
                device_id={axis: peer},
                device_id_type=MESH,
            )
            copy.start()
            copies.append(copy)
        return copies

    def arrived(copies):
        for copy in copies:
            copy.wait_recv()

    picks = (
        lax.broadcasted_iota(jnp.int32, (dense_pad, dense), 0)
        == lax.broadcasted_iota(jnp.int32, (dense_pad, dense), 1)
    ).astype(F32).astype(BF16)
    dense_t = contract(picks, dense_ref[...], 1, 1).astype(BF16)
    ids = lax.broadcasted_iota(jnp.int32, (uniq, local), 0)
    rows_bf = rows_ref[0]
    for k in range(ngrp):
        lanes = slice(k * local, (k + 1) * local)
        total = jnp.zeros((uniq, local), F32)
        for j in range(bag):
            wanted = jnp.where(j < length_ref[:, lanes], index_ref[0, j : j + 1, lanes], -1)
            total = total + jnp.where(ids == wanted, 1.0, 0.0)
        counts[:, lanes] = total.astype(BF16)
        pool_out[k, :width, :] = contract(rows_bf, counts[:, lanes], 0, 0).astype(BF16)
        pool_out[k, width:, :] = dense_t
    pl.semaphore_wait(barrier, ngrp - 1 + ncol - 1)
    pool_copies = send("grp", ngrp, grp, lambda p: pool_out.at[p], pool_in, pool_s, pool_r)
    pool_in[grp] = pool_out[grp]

    weight_pad[...] = jnp.zeros_like(weight_pad)
    weight_pad[:dense, :] = bottom_ref[...]
    weight = weight_pad[...]
    pre[...] = contract(weight, dense_t, 0, 0)
    bottom = jax.nn.silu(pre[...]).astype(BF16)
    spread_out[:emb, :] = bottom
    spread_out[emb:, :] = jnp.zeros((pair_pad, local), BF16)
    base[...] = contract(top_ref[:emb, :], bottom, 0, 0)
    own = pl.ds(pl.multiple_of(col * width, width), width)
    vec[0] = spread_out[own, :].astype(F32)
    out_column = contract(out_ref[...], jnp.ones((1, local), BF16), 0, 0)
    back_out[:, width:, :] = jnp.zeros((ngrp, dense_pad, local), BF16)
    top_out[:, piece + pair_pad :, :] = jnp.zeros((ngrp, 16, local), BF16)
    delta_out[:, width:, :] = jnp.zeros((ncol, pair_pad, local), BF16)

    holders = []
    for f in range(ngrp):
        holder = jnp.int32(0)
        for k in range(ngrp):
            holder = jnp.where(slot_ref[k] == f, k, holder)
        holders.append(holder)
    arrived(pool_copies)
    for f in range(ngrp):
        vec[1 + f] = pool_in[holders[f], :width, :].astype(F32)
    for i, (a, b) in enumerate(pairs):
        gram_in[col, i : i + 1, :] = jnp.sum(vec[a] * vec[b], axis=0, keepdims=True)
    gram_copies = send("col", ncol, col, lambda p: gram_in.at[col], gram_in, gram_s, gram_r)

    for k in range(ngrp):
        bottoms[:, k * local : (k + 1) * local] = jax.nn.silu(
            contract(weight, pool_in[k, width:, :], 0, 0)
        ).astype(BF16)

    arrived(gram_copies)
    gram = gram_in[0, :npairs, :]
    for c in range(1, ncol):
        gram = gram + gram_in[c, :npairs, :]
    spread_out[emb : emb + npairs, :] = gram.astype(BF16)
    pair_t = spread_out[emb : emb + npairs, :]
    hidden_pre = base[...] + contract(top_ref[emb:, :], pair_t, 0, 0)
    sigma = jax.nn.sigmoid(hidden_pre)
    hid[...] = (hidden_pre * sigma).astype(BF16)
    logit_in[col, :, :] = jnp.broadcast_to(
        contract(out_ref[...], hid[...], 1, 0), (8, local)
    )
    logit_copies = send("col", ncol, col, lambda p: logit_in.at[col], logit_in, logit_s, logit_r)
    base[...] = out_column * (sigma * (1.0 + hidden_pre * (1.0 - sigma)))
    for k in range(ngrp):
        top_out[k, piece : piece + pair_pad, :] = spread_out[emb:, :]
    arrived(logit_copies)
    logits = logit_in[0, 0:1, :]
    for c in range(1, ncol):
        logits = logits + logit_in[c, 0:1, :]
    logits_ref[...] = logits
    dlogit = (jax.nn.sigmoid(logits) - label_ref[...].astype(F32)) / local
    delta = (dlogit * base[...]).astype(BF16)
    dfeatures = contract(top_ref[...], delta, 1, 0)
    for c in range(ncol):
        delta_out[c, :width, :] = dfeatures[c * width : (c + 1) * width, :].astype(BF16)
        delta_out[c, width : width + npairs, :] = dfeatures[emb:, :].astype(BF16)
    delta_copies = send(
        "col", ncol, col, lambda p: delta_out.at[p], delta_in, delta_s, delta_r
    )
    delta_in[col] = delta_out[col]
    dlogit_rows = split_rows(dlogit, 3)
    for k in range(ngrp):
        top_out[k, :piece, :] = delta[k * piece : (k + 1) * piece, :]
        share = contract(dlogit_rows, hid[k * piece : (k + 1) * piece, :], 1, 1)
        top_out[k, piece + pair_pad :, :piece] = split_rows(
            jnp.sum(share, axis=0, keepdims=True), 3
        )
    top_copies = send("grp", ngrp, grp, lambda p: top_out.at[p], top_in, top_s, top_r)
    top_in[grp] = top_out[grp]

    own_pre = pre[own, :]
    own_sigma = jax.nn.sigmoid(own_pre)
    own_slope = own_sigma * (1.0 + own_pre * (1.0 - own_sigma))
    arrived(delta_copies)
    arriving = delta_in[0].astype(F32)
    for c in range(1, ncol):
        arriving = arriving + delta_in[c].astype(F32)
    dpairs = arriving[width:, :].astype(BF16).astype(F32)
    where = {}
    for i, (a, b) in enumerate(pairs):
        where[a, b] = where[b, a] = i
    for a in range(fields):
        total = jnp.zeros((width, local), F32)
        for b in range(fields):
            if a != b:
                i = where[a, b]
                total = total + dpairs[i : i + 1, :] * vec[b]
        if a == 0:
            dbottom = (arriving[:width, :] + total) * own_slope
        else:
            dvec[a - 1] = total.astype(BF16)
    rest, bottom_part = dbottom, jnp.zeros((dense_pad, width), F32)
    for part in range(3):
        head = rest.astype(BF16)
        bottom_part = bottom_part + contract(dense_t, head, 1, 1)
        rest = rest - head.astype(F32)
    bottom_part = bottom_part.astype(BF16)
    for k in range(ngrp):
        back_out[k, :width, :] = dvec[slot_ref[k]]
        back_out[k, width:, :width] = bottom_part
    back_copies = send("grp", ngrp, grp, lambda p: back_out.at[p], back_in, back_s, back_r)
    back_in[grp] = back_out[grp]

    arrived(top_copies)
    deltas = side_by_side(top_in, ngrp, slice(0, piece))
    grad_top_ref[:emb, :] = contract(bottoms[...], deltas, 1, 1)
    grad_top_ref[emb:, :] = contract(
        side_by_side(top_in, ngrp, slice(piece, piece + pair_pad)), deltas, 1, 1
    )[:npairs, :]
    out_rows = top_in[0, piece + pair_pad :, :].astype(F32)
    for k in range(1, ngrp):
        out_rows = out_rows + top_in[k, piece + pair_pad :, :].astype(F32)
    grad_out_ref[...] = jnp.sum(out_rows, axis=0, keepdims=True)[:, :piece]

    arrived(back_copies)
    corner = back_in[0, width:, :].astype(F32)
    for k in range(1, ngrp):
        corner = corner + back_in[k, width:, :].astype(F32)
    corner_in[col] = corner
    corner_copies = send(
        "col", ncol, col, lambda p: corner_in.at[col], corner_in, corner_s, corner_r
    )
    grad_rows_ref[0] = contract(
        counts[...], side_by_side(back_in, ngrp, slice(0, width)), 1, 1
    )
    arrived(corner_copies)
    grad_bottom_ref[...] = jnp.concatenate(
        [corner_in[c, :dense, :width] for c in range(ncol)], axis=1
    )
    for copies in (
        pool_copies, gram_copies, logit_copies, delta_copies, top_copies, back_copies, corner_copies
    ):
        for copy in copies:
            copy.wait_send()


def fused(ncol, ngrp, table_rows, pool_index, bag_length, table_slot, dense_input, bottom_weight,
          top_weight, out_weight, labels):
    uniq, width = table_rows.shape[1:]
    samples = pool_index.shape[2]
    local, dense = dense_input.shape
    emb = bottom_weight.shape[1]
    topin, hidden_count = top_weight.shape
    piece = hidden_count // ngrp
    npairs = topin - emb
    pair_pad, dense_pad = up(npairs, 16), up(dense, 16)
    shape = jax.ShapeDtypeStruct
    vmem = pl.BlockSpec(memory_space=pltpu.VMEM)
    dma = pltpu.SemaphoreType.DMA
    sems = []
    for count in (ngrp, ncol, ncol, ngrp, ncol, ngrp, ncol):
        sems += [dma((count,)), dma((count,))]
    made = pl.pallas_call(
        functools.partial(kernel, ncol, ngrp),
        out_shape=(
            shape((1, local), F32),
            shape((topin, piece), F32),
            shape((1, piece), F32),
            shape((dense, emb), F32),
            shape((1, uniq, width), F32),
        ),
        in_specs=[pl.BlockSpec(memory_space=pltpu.SMEM)] + [vmem] * 8,
        out_specs=(vmem,) * 5,
        scratch_shapes=[
            pltpu.VMEM((uniq, samples), BF16),
            pltpu.VMEM((ngrp, width + dense_pad, local), BF16),
            pltpu.VMEM((ngrp, width + dense_pad, local), BF16),
            pltpu.VMEM((dense_pad, emb), BF16),
            pltpu.VMEM((emb, local), F32),
            pltpu.VMEM((emb, samples), BF16),
            pltpu.VMEM((hidden_count, local), F32),
            pltpu.VMEM((emb + pair_pad, local), BF16),
            pltpu.VMEM((ngrp + 1, width, local), F32),
            pltpu.VMEM((ncol, up(npairs, 8), local), F32),
            pltpu.VMEM((hidden_count, local), BF16),
            pltpu.VMEM((ncol, 8, local), F32),
            pltpu.VMEM((ngrp, piece + pair_pad + 16, local), BF16),
            pltpu.VMEM((ngrp, piece + pair_pad + 16, local), BF16),
            pltpu.VMEM((ncol, width + pair_pad, local), BF16),
            pltpu.VMEM((ncol, width + pair_pad, local), BF16),
            pltpu.VMEM((ngrp, width, local), BF16),
            pltpu.VMEM((ngrp, width + dense_pad, local), BF16),
            pltpu.VMEM((ngrp, width + dense_pad, local), BF16),
            pltpu.VMEM((ncol, dense_pad, local), F32),
        ] + sems,
        compiler_params=pltpu.CompilerParams(
            collective_id=0, has_side_effects=True, vmem_limit_bytes=32 * 2**20
        ),
    )(
        table_slot, table_rows, pool_index, bag_length, dense_input, bottom_weight, top_weight,
        out_weight.reshape(1, -1), labels.reshape(1, -1),
    )
    logits, grad_top, grad_out, grad_bottom, grad_rows = made
    return logits.reshape(-1), grad_top, grad_out.reshape(-1), grad_bottom, grad_rows


def choose(ncol, ngrp, *arrays):
    table_rows, dense_input, top_weight = arrays[0], arrays[4], arrays[6]
    local, width, piece = dense_input.shape[0], table_rows.shape[2], top_weight.shape[1] // ngrp
    fits = (
        table_rows.shape[0] == 1
        and (ngrp + 1) * ngrp // 2 <= UNROLLED_PAIRS
        and local % 128 == 0
        and width % 16 == 0 and width <= local
        and piece % 16 == 0 and piece <= local
    )
    return fused(ncol, ngrp, *arrays) if fits else body(*arrays)


def solution(mesh):
    placed = (
        P("grp", None, "col"),
        P("grp", None, None),
        P("grp", None),
        P(),
        P("grp", None),
        P(),
        P(None, "col"),
        P("col"),
        P("grp"),
    )
    return jax.shard_map(
        functools.partial(choose, mesh.shape["col"], mesh.shape["grp"]),
        mesh=mesh,
        in_specs=placed,
        out_specs=(
            P("grp"),
            P(None, ("col", "grp")),
            P(("col", "grp")),
            P(),
            P("grp", None, "col"),
        ),
        check_vma=False,
    )
```

```python
import functools

import jax
import jax.numpy as jnp
import numpy as np
from jax import lax
from jax.experimental import pallas as pl
from jax.experimental.pallas import tpu as pltpu
from jax.sharding import PartitionSpec as P


def count_block(index_block, length_block, uniq_count):
    slot_iota = lax.broadcasted_iota(jnp.int32, index_block.shape, 1)
    row_ids = jnp.where(slot_iota < length_block[:, None, :], index_block, -1)
    values = lax.broadcasted_iota(jnp.int32, (1, 1, uniq_count), 2)
    counts = jnp.zeros((index_block.shape[0], index_block.shape[2], uniq_count), jnp.bfloat16)
    for slot_index in range(index_block.shape[1]):
        counts = counts + jnp.where(row_ids[:, slot_index, :, None] == values, 1.0, 0.0).astype(
            jnp.bfloat16
        )
    return counts


def pair_table(fields):
    upper_a, upper_b = np.triu_indices(fields, 1)
    return upper_a * fields + upper_b


def silu_slope(values):
    sigma = jax.nn.sigmoid(values)
    return sigma * (1.0 + values * (1.0 - sigma))


def interact(vectors):
    fields = vectors.shape[0]
    gram_matrix = jnp.einsum("asc,bsc->abs", vectors, vectors, preferred_element_type=jnp.float32)
    return gram_matrix.reshape(fields * fields, -1)[pair_table(fields)]


def spread(dpairs, vectors):
    fields = vectors.shape[0]
    symmetric = (
        jnp.zeros((fields * fields, dpairs.shape[0]), jnp.bfloat16)
        .at[pair_table(fields)]
        .set(dpairs.T)
    )
    symmetric = symmetric.reshape(fields, fields, -1)
    symmetric = symmetric + jnp.transpose(symmetric, (1, 0, 2))
    return jnp.einsum("abs,bsc->asc", symmetric, vectors, preferred_element_type=jnp.float32)


def body(
    table_rows,
    pool_index,
    bag_length,
    table_slot,
    dense_input,
    bottom_weight,
    top_weight,
    out_weight,
    labels,
):
    tab_count, uniq_count, col_width = table_rows.shape
    bag_slots = pool_index.shape[1]
    samples = pool_index.shape[2]
    local_rows = dense_input.shape[0]
    emb_width = bottom_weight.shape[1]
    stride = min(1024, samples)
    nblocks = samples // stride
    index_blocks = jnp.transpose(
        pool_index.reshape(tab_count, bag_slots, nblocks, stride), (2, 0, 1, 3)
    )
    length_blocks = jnp.transpose(bag_length.reshape(tab_count, nblocks, stride), (1, 0, 2))

    def pool_one(inputs):
        counts = count_block(inputs[0], inputs[1], uniq_count)
        return jnp.einsum(
            "tbu,tuc->tbc", counts, table_rows, preferred_element_type=jnp.float32
        ).astype(jnp.bfloat16)

    pooled_blocks = lax.map(pool_one, (index_blocks, length_blocks))
    pooled = jnp.transpose(pooled_blocks, (1, 0, 2, 3)).reshape(tab_count, samples, col_width)
    picks = (
        lax.broadcasted_iota(jnp.int32, (table_slot.shape[0],) * 2, 0) == table_slot[None, :]
    ).astype(jnp.bfloat16)
    bottom_pre = jnp.dot(dense_input, bottom_weight, preferred_element_type=jnp.float32)
    bottom_out = jax.nn.silu(bottom_pre).astype(jnp.bfloat16)
    arrived = lax.all_to_all(pooled, "grp", split_axis=1, concat_axis=0, tiled=True)
    gathered = lax.all_gather(arrived, "col", axis=2, tiled=True)
    tables = jnp.einsum(
        "fk,ksc->fsc", picks, gathered, preferred_element_type=jnp.float32
    ).astype(jnp.bfloat16)
    mine_pre, mine_out, mine_dense = (bottom_pre, bottom_out, dense_input)
    vectors = jnp.concatenate([mine_out[None], tables], axis=0)
    pair_values = interact(vectors)
    features = jnp.concatenate([mine_out.astype(jnp.float32), pair_values.T], axis=1).astype(
        jnp.bfloat16
    )
    hidden_pre = jnp.dot(features, top_weight, preferred_element_type=jnp.float32)
    hidden = jax.nn.silu(hidden_pre).astype(jnp.bfloat16)
    logits = lax.psum(jnp.dot(hidden, out_weight, preferred_element_type=jnp.float32), "col")
    dlogit = (jax.nn.sigmoid(logits) - labels.astype(jnp.float32)) / local_rows
    grad_out_part = jnp.dot(hidden.astype(jnp.float32).T, dlogit, precision=lax.Precision.HIGHEST)
    out_delta = (
        dlogit[:, None] * out_weight.astype(jnp.float32)[None, :] * silu_slope(hidden_pre)
    ).astype(jnp.bfloat16)
    grad_top_part = lax.dot_general(
        features, out_delta, (((0,), (0,)), ((), ())), preferred_element_type=jnp.float32
    )
    grad_top, grad_out = (
        lax.psum_scatter(grad_top_part, "grp", scatter_dimension=1, tiled=True),
        lax.psum_scatter(grad_out_part, "grp", scatter_dimension=0, tiled=True),
    )
    dfeatures = lax.psum(
        lax.dot_general(
            out_delta, top_weight, (((1,), (1,)), ((), ())), preferred_element_type=jnp.float32
        ),
        "col",
    )
    dpairs = dfeatures[:, emb_width:].astype(jnp.bfloat16)
    dvectors = spread(dpairs, vectors)
    dbottom = (dfeatures[:, :emb_width] + dvectors[0]) * silu_slope(mine_pre)
    bottom_part = jnp.dot(
        mine_dense.astype(jnp.float32).T, dbottom, precision=lax.Precision.HIGHEST
    )
    dtables = jnp.einsum(
        "fk,fsc->ksc",
        picks,
        dvectors[1:].astype(jnp.bfloat16),
        preferred_element_type=jnp.float32,
    )
    grad_bottom = lax.psum(bottom_part, "grp")
    own_cols = lax.dynamic_slice_in_dim(
        dtables, lax.axis_index("col") * col_width, col_width, 2
    ).astype(jnp.bfloat16)
    dpooled = lax.all_to_all(own_cols, "grp", split_axis=0, concat_axis=1, tiled=True)
    dpooled_blocks = jnp.transpose(
        dpooled.reshape(tab_count, nblocks, stride, col_width), (1, 0, 2, 3)
    )

    def accumulate(running, inputs):
        counts = count_block(inputs[0], inputs[1], uniq_count)
        return (
            running
            + jnp.einsum("tbu,tbc->tuc", counts, inputs[2], preferred_element_type=jnp.float32),
            None,
        )

    grad_rows, _ = lax.scan(
        accumulate,
        jnp.zeros((tab_count, uniq_count, col_width), jnp.float32),
        (index_blocks, length_blocks, dpooled_blocks),
    )
    return (logits, grad_top, grad_out, grad_bottom, grad_rows)


MESH = pl.DeviceIdType.MESH
F32, BF16 = jnp.float32, jnp.bfloat16
UNROLLED_PAIRS = 128


def contract(left, right, left_dim, right_dim):
    return lax.dot_general(
        left, right, (((left_dim,), (right_dim,)), ((), ())), preferred_element_type=F32
    )


def up(count, unit):
    return -(-count // unit) * unit


def side_by_side(ref, count, rows):
    return jnp.concatenate([ref[k, rows, :] for k in range(count)], axis=1)


def split_rows(values, parts):
    row = lax.broadcasted_iota(jnp.int32, (16, values.shape[1]), 0)
    block = jnp.zeros((16, values.shape[1]), F32)
    rest = values
    for part in range(parts):
        head = rest.astype(BF16).astype(F32)
        block = jnp.where(row == part, head, block)
        rest = rest - head
    return block.astype(BF16)


def kernel(
    ncol, ngrp,
    slot_ref, rows_ref, index_ref, length_ref, dense_ref, bottom_ref, top_hbm, out_ref, label_ref,
    logits_ref, grad_top_ref, grad_out_ref, grad_bottom_ref, grad_rows_ref,
    counts, pool_out, pool_in, weight_pad, pre, bottoms, base, spread_out, vec, gram_in,
    hid, top_out, top_in, delta_out, delta_in, dvec, back_out, back_in, corner_in,
    pool_s, pool_r, gram_s, gram_r, delta_s, delta_r,
    top_s, top_r, back_s, back_r, corner_s, corner_r, top_ref, load_sem, dense_rows,
):
    col, grp = lax.axis_index("col"), lax.axis_index("grp")
    width, uniq = rows_ref.shape[1], rows_ref.shape[2]
    bag, samples = index_ref.shape[1], index_ref.shape[2]
    dense, local = dense_ref.shape
    emb = bottom_ref.shape[1]
    hidden_count = top_ref.shape[1]
    piece = hidden_count // ngrp
    fields = ngrp + 1
    pairs = [(a, b) for a in range(fields) for b in range(a + 1, fields)]
    npairs = len(pairs)
    pair_pad = up(npairs, 16)
    dense_pad = up(dense, 16)

    top_load = pltpu.make_async_copy(top_hbm, top_ref, load_sem)
    top_load.start()
    barrier = pltpu.get_barrier_semaphore()
    for d in range(1, ngrp):
        pl.semaphore_signal(
            barrier, inc=1, device_id={"grp": lax.rem(grp + d, ngrp)}, device_id_type=MESH
        )
    for d in range(1, ncol):
        pl.semaphore_signal(
            barrier, inc=1, device_id={"col": lax.rem(col + d, ncol)}, device_id_type=MESH
        )

    def send(axis, count, here, source, target, send_sem, recv_sem):
        copies = []
        for d in range(1, count):
            peer = lax.rem(here + d, count)
            copy = pltpu.make_async_remote_copy(
                src_ref=source(peer),
                dst_ref=target.at[here],
                send_sem=send_sem.at[d],
                recv_sem=recv_sem.at[d],
                device_id={axis: peer},
                device_id_type=MESH,
            )
            copy.start()
            copies.append(copy)
        return copies

    def arrived(copies):
        for copy in copies:
            copy.wait_recv()

    out_row = out_ref[...].reshape(1, hidden_count)
    dense_rows[...] = jnp.zeros_like(dense_rows)
    dense_rows[:dense, :] = dense_ref[...]
    dense_t = dense_rows[...]
    ids = lax.broadcasted_iota(jnp.int32, (uniq, local), 0)
    rows_bf = rows_ref[0]
    for k in range(ngrp):
        lanes = slice(k * local, (k + 1) * local)
        total = jnp.zeros((uniq, local), F32)
        for j in range(bag):
            wanted = jnp.where(j < length_ref[:, lanes], index_ref[0, j : j + 1, lanes], -1)
            total = total + jnp.where(ids == wanted, 1.0, 0.0)
        counts[:, lanes] = total.astype(BF16)
        pool_out[k, :width, :] = contract(rows_bf, counts[:, lanes], 1, 0).astype(BF16)
        pool_out[k, width:, :] = dense_t
    pl.semaphore_wait(barrier, ngrp - 1 + ncol - 1)
    pool_copies = send("grp", ngrp, grp, lambda p: pool_out.at[p], pool_in, pool_s, pool_r)
    pool_in[grp] = pool_out[grp]

    weight_pad[...] = jnp.zeros_like(weight_pad)
    weight_pad[:dense, :] = bottom_ref[...]
    weight = weight_pad[...]
    pre[...] = contract(weight, dense_t, 0, 0)
    bottom = jax.nn.silu(pre[...]).astype(BF16)
    spread_out[:emb, :] = bottom
    spread_out[emb:, :] = jnp.zeros((pair_pad, local), BF16)
    top_load.wait()
    base[...] = contract(top_ref[:emb, :], bottom, 0, 0)
    own = pl.ds(pl.multiple_of(col * width, width), width)
    vec[0] = spread_out[own, :].astype(F32)
    out_column = contract(out_row, jnp.ones((1, local), BF16), 0, 0)
    back_out[:, width:, :] = jnp.zeros((ngrp, dense_pad, local), BF16)
    top_out[:, piece + pair_pad :, :] = jnp.zeros((ngrp, 16, local), BF16)
    delta_out[:, width : width + pair_pad, :] = jnp.zeros((ncol, pair_pad, local), BF16)

    holders = []
    for f in range(ngrp):
        holder = jnp.int32(0)
        for k in range(ngrp):
            holder = jnp.where(slot_ref[k] == f, k, holder)
        holders.append(holder)
    arrived(pool_copies)
    for f in range(ngrp):
        vec[1 + f] = pool_in[holders[f], :width, :].astype(F32)
    for i, (a, b) in enumerate(pairs):
        gram_in[col, i : i + 1, :] = jnp.sum(vec[a] * vec[b], axis=0, keepdims=True)
    gram_copies = send("col", ncol, col, lambda p: gram_in.at[col], gram_in, gram_s, gram_r)

    for k in range(ngrp):
        bottoms[:, k * local : (k + 1) * local] = jax.nn.silu(
            contract(weight, pool_in[k, width:, :], 0, 0)
        ).astype(BF16)

    arrived(gram_copies)
    gram = gram_in[0, :npairs, :]
    for c in range(1, ncol):
        gram = gram + gram_in[c, :npairs, :]
    spread_out[emb : emb + npairs, :] = gram.astype(BF16)
    pair_t = spread_out[emb : emb + npairs, :]
    hidden_pre = base[...] + contract(top_ref[emb:, :], pair_t, 0, 0)
    sigma = jax.nn.sigmoid(hidden_pre)
    hid[...] = (hidden_pre * sigma).astype(BF16)
    base[...] = out_column * (sigma * (1.0 + hidden_pre * (1.0 - sigma)))
    for k in range(ngrp):
        top_out[k, piece : piece + pair_pad, :] = spread_out[emb:, :]
    dfeatures = contract(top_ref[...], base[...].astype(BF16), 1, 0)
    logit_rows = split_rows(contract(out_row, hid[...], 1, 0), 3)
    for c in range(ncol):
        delta_out[c, :width, :] = dfeatures[c * width : (c + 1) * width, :].astype(BF16)
        delta_out[c, width : width + npairs, :] = dfeatures[emb:, :].astype(BF16)
        delta_out[c, width + pair_pad :, :] = logit_rows
    delta_copies = send(
        "col", ncol, col, lambda p: delta_out.at[p], delta_in, delta_s, delta_r
    )
    delta_in[col] = delta_out[col]
    own_pre = pre[own, :]
    own_sigma = jax.nn.sigmoid(own_pre)
    own_slope = own_sigma * (1.0 + own_pre * (1.0 - own_sigma))
    arrived(delta_copies)
    arriving = delta_in[0].astype(F32)
    for c in range(1, ncol):
        arriving = arriving + delta_in[c].astype(F32)
    logits = jnp.sum(arriving[width + pair_pad :, :], axis=0, keepdims=True)
    logits_ref[...] = logits
    dlogit = (jax.nn.sigmoid(logits) - label_ref[...].astype(F32)) / local
    dpairs = (arriving[width : width + pair_pad, :] * dlogit).astype(BF16).astype(F32)
    where = {}
    for i, (a, b) in enumerate(pairs):
        where[a, b] = where[b, a] = i
    for a in range(fields):
        total = jnp.zeros((width, local), F32)
        for b in range(fields):
            if a != b:
                i = where[a, b]
                total = total + dpairs[i : i + 1, :] * vec[b]
        if a == 0:
            dbottom = (arriving[:width, :] * dlogit + total) * own_slope
        else:
            dvec[a - 1] = total.astype(BF16)
    rest, bottom_part = dbottom, jnp.zeros((dense_pad, width), F32)
    for part in range(3):
        head = rest.astype(BF16)
        bottom_part = bottom_part + contract(dense_t, head, 1, 1)
        rest = rest - head.astype(F32)
    bottom_part = bottom_part.astype(BF16)
    for k in range(ngrp):
        back_out[k, :width, :] = dvec[slot_ref[k]]
        back_out[k, width:, :width] = bottom_part
    back_copies = send("grp", ngrp, grp, lambda p: back_out.at[p], back_in, back_s, back_r)
    back_in[grp] = back_out[grp]

    delta = (dlogit * base[...]).astype(BF16)
    dlogit_rows = split_rows(dlogit, 3)
    for k in range(ngrp):
        top_out[k, :piece, :] = delta[k * piece : (k + 1) * piece, :]
        share = contract(dlogit_rows, hid[k * piece : (k + 1) * piece, :], 1, 1)
        top_out[k, piece + pair_pad :, :piece] = split_rows(
            jnp.sum(share, axis=0, keepdims=True), 3
        )
    top_copies = send("grp", ngrp, grp, lambda p: top_out.at[p], top_in, top_s, top_r)
    top_in[grp] = top_out[grp]

    arrived(top_copies)
    deltas = side_by_side(top_in, ngrp, slice(0, piece))
    grad_top_ref[:, :emb] = contract(deltas, bottoms[...], 1, 1)
    grad_top_ref[:, emb:] = contract(
        deltas, side_by_side(top_in, ngrp, slice(piece, piece + pair_pad)), 1, 1
    )[:, :npairs]
    out_rows = top_in[0, piece + pair_pad :, :].astype(F32)
    for k in range(1, ngrp):
        out_rows = out_rows + top_in[k, piece + pair_pad :, :].astype(F32)
    grad_out_ref[...] = jnp.sum(out_rows, axis=0, keepdims=True)[:, :piece]

    arrived(back_copies)
    corner = back_in[0, width:, :].astype(F32)
    for k in range(1, ngrp):
        corner = corner + back_in[k, width:, :].astype(F32)
    corner_in[col] = corner
    corner_copies = send(
        "col", ncol, col, lambda p: corner_in.at[col], corner_in, corner_s, corner_r
    )
    grad_rows_ref[0] = contract(
        side_by_side(back_in, ngrp, slice(0, width)), counts[...], 1, 1
    )
    arrived(corner_copies)
    grad_bottom_ref[...] = jnp.concatenate(
        [corner_in[c, :dense, :width] for c in range(ncol)], axis=1
    )
    for copies in (
        pool_copies, gram_copies, delta_copies, top_copies, back_copies, corner_copies
    ):
        for copy in copies:
            copy.wait_send()


def hand_over(*refs):
    half = len(refs) // 2
    for made, result in zip(refs[:half], refs[half:]):
        result[...] = made[...]


def fused(ncol, ngrp, table_rows, pool_index, bag_length, table_slot, dense_input, bottom_weight,
          top_weight, out_weight, labels):
    uniq, width = table_rows.shape[1:]
    samples = pool_index.shape[2]
    local, dense = dense_input.shape
    emb = bottom_weight.shape[1]
    topin, hidden_count = top_weight.shape
    piece = hidden_count // ngrp
    npairs = topin - emb
    pair_pad, dense_pad = up(npairs, 16), up(dense, 16)
    shape = jax.ShapeDtypeStruct
    vmem = pl.BlockSpec(memory_space=pltpu.VMEM)
    dma = pltpu.SemaphoreType.DMA
    sems = []
    for count in (ngrp, ncol, ncol, ngrp, ngrp, ncol):
        sems += [dma((count,)), dma((count,))]
    made = pl.pallas_call(
        functools.partial(kernel, ncol, ngrp),
        out_shape=(
            shape((1, local), F32),
            shape((piece, topin), F32),
            shape((1, piece), F32),
            shape((dense, emb), F32),
            shape((1, width, uniq), F32),
        ),
        in_specs=[pl.BlockSpec(memory_space=pltpu.SMEM)] + [vmem] * 5
        + [pl.BlockSpec(memory_space=pltpu.HBM)] + [vmem] * 2,
        out_specs=(vmem,) * 5,
        scratch_shapes=[
            pltpu.VMEM((uniq, samples), BF16),
            pltpu.VMEM((ngrp, width + dense_pad, local), BF16),
            pltpu.VMEM((ngrp, width + dense_pad, local), BF16),
            pltpu.VMEM((dense_pad, emb), BF16),
            pltpu.VMEM((emb, local), F32),
            pltpu.VMEM((emb, samples), BF16),
            pltpu.VMEM((hidden_count, local), F32),
            pltpu.VMEM((emb + pair_pad, local), BF16),
            pltpu.VMEM((ngrp + 1, width, local), F32),
            pltpu.VMEM((ncol, up(npairs, 8), local), F32),
            pltpu.VMEM((hidden_count, local), BF16),
            pltpu.VMEM((ngrp, piece + pair_pad + 16, local), BF16),
            pltpu.VMEM((ngrp, piece + pair_pad + 16, local), BF16),
            pltpu.VMEM((ncol, width + pair_pad + 16, local), BF16),
            pltpu.VMEM((ncol, width + pair_pad + 16, local), BF16),
            pltpu.VMEM((ngrp, width, local), BF16),
            pltpu.VMEM((ngrp, width + dense_pad, local), BF16),
            pltpu.VMEM((ngrp, width + dense_pad, local), BF16),
            pltpu.VMEM((ncol, dense_pad, local), F32),
        ] + sems + [
            pltpu.VMEM((topin, hidden_count), BF16),
            pltpu.SemaphoreType.DMA,
            pltpu.VMEM((dense_pad, local), BF16),
        ],
        compiler_params=pltpu.CompilerParams(
            collective_id=0, has_side_effects=True, vmem_limit_bytes=60 * 2**20
        ),
    )(
        table_slot, jnp.swapaxes(table_rows, 1, 2), pool_index, bag_length, dense_input.T,
        bottom_weight, top_weight, out_weight, labels.reshape(1, -1),
    )
    logits, grad_top, grad_out, grad_bottom, grad_rows = pl.pallas_call(
        hand_over,
        out_shape=tuple(shape(a.shape, a.dtype) for a in made),
        in_specs=[vmem] * 5,
        out_specs=(vmem,) * 5,
        compiler_params=pltpu.CompilerParams(vmem_limit_bytes=60 * 2**20),
    )(*made)
    return (
        logits.reshape(-1), grad_top.T, grad_out.reshape(-1), grad_bottom,
        jnp.swapaxes(grad_rows, 1, 2),
    )


def choose(ncol, ngrp, *arrays):
    table_rows, dense_input, top_weight = arrays[0], arrays[4], arrays[6]
    local, width, piece = dense_input.shape[0], table_rows.shape[2], top_weight.shape[1] // ngrp
    fits = (
        table_rows.shape[0] == 1
        and (ngrp + 1) * ngrp // 2 <= UNROLLED_PAIRS
        and local % 128 == 0
        and width % 16 == 0 and width <= local
        and piece % 16 == 0 and piece <= local
    )
    return fused(ncol, ngrp, *arrays) if fits else body(*arrays)


def solution(mesh):
    placed = (
        P("grp", None, "col"),
        P("grp", None, None),
        P("grp", None),
        P(),
        P("grp", None),
        P(),
        P(None, "col"),
        P("col"),
        P("grp"),
    )
    return jax.shard_map(
        functools.partial(choose, mesh.shape["col"], mesh.shape["grp"]),
        mesh=mesh,
        in_specs=placed,
        out_specs=(
            P("grp"),
            P(None, ("col", "grp")),
            P(("col", "grp")),
            P(),
            P("grp", None, "col"),
        ),
        check_vma=False,
    )
```
